32 devices in a mesh: gx: 8 (over z, core), gy: 4 (over y, x).
Axes of the slice: x: 2, y: 2, z: 4, core: 2. Of those that a mesh axis runs over, the one named last changes fastest.
Arguments:
- source: float32 [64, 64, 128], P('gx', 'gy'), may hold values from -6 to 6, as said below
- coupling_x: float32 [64, 64, 128], P('gx', 'gy'), may hold values from 128 to 512
- coupling_y: float32 [64, 64, 128], P('gx', 'gy'), may hold values from 128 to 512
- reaction: float32 [64, 64, 128], P('gx', 'gy'), may hold values from 0.03 to 0.12
Outputs:
- advanced: float32 [64, 64, 128], P('gx', 'gy')
The draws below stay inside these ranges and needn't reach their ends.
Inputs may be any that keep to these rules, and one draw needn't show every extreme that they name: source terms of the sub-step.
All inputs are finite; a program needn't handle non-finite values.
Results may differ from the reference program's by a relative error of at most 0.002.
Values sent between devices are 32-bit elements; how exact they have to be, the bound alone decides.
A program may use at most 64 MiB of HBM per device.

```python
import math
import jax
import jax.numpy as jnp
from jax import lax

NZ = 128
NX = 64
NY = 64


def draw_source(key, part):
    shape = (NX, NY, NZ)
    values = jax.random.truncated_normal(key, -6.0, 6.0, shape, jnp.float32)
    return values


def levels(stream_key, extent, split, low, top_value):
    gain, own = 1.0, jax.random.fold_in(stream_key, 6)
    for dim, blocks in split:
        steps = jnp.exp(jax.random.uniform(jax.random.fold_in(own, dim), (blocks,), jnp.float32, low / len(split), top_value / len(split)))
        gain = gain * jnp.repeat(steps, extent[dim] // blocks).reshape([-1 if axis == dim else 1 for axis in range(len(extent))])
    return gain


def setup_inputs(seed: int = 0) -> dict:
    key_list = jax.random.split(jax.random.key(seed), 5)
    source = draw_source(jax.random.fold_in(key_list[4], 71), 0)
    coupling_x = jnp.clip(jnp.exp(math.log(512.0) - 1.3862944 * jax.random.uniform(key_list[1], (NX, NY, NZ), jnp.float32) ** levels(key_list[1], (NX, NY, NZ), ((0, 8), (1, 4)), -0.2, 0.2)), 128.0, 512.0)
    coupling_y = jnp.clip(jnp.exp(math.log(512.0) - 1.3862944 * jax.random.uniform(key_list[2], (NX, NY, NZ), jnp.float32) ** levels(key_list[2], (NX, NY, NZ), ((0, 8), (1, 4)), -0.2, 0.2)), 128.0, 512.0)
    reaction = jnp.clip(jnp.exp(math.log(0.12) - 1.3862944 * jax.random.uniform(key_list[3], (NX, NY, NZ), jnp.float32) ** levels(key_list[3], (NX, NY, NZ), ((0, 8), (1, 4)), -0.2, 0.2)), 0.03, 0.12)
    return {"source": source, "coupling_x": coupling_x, "coupling_y": coupling_y, "reaction": reaction}


def sweep(source, neighbor_coupling, reaction):
    zero_row = jnp.zeros_like(source[0])

    def forward_step(carry, cells):
        ratio_prev, shifted_prev = carry
        value, link, decay = cells
        denom = decay + 2.0 * link + link * ratio_prev
        ratio_now = -link / denom
        shifted_now = (value + link * shifted_prev) / denom
        return (ratio_now, shifted_now), (ratio_now, shifted_now)

    final_carry, outputs = lax.scan(forward_step, (zero_row, zero_row), (source, neighbor_coupling, reaction))

    def backward_step(later_value, cells):
        ratio_now, shifted_now = cells
        current = shifted_now - ratio_now * later_value
        return current, current

    last_carry, solved = lax.scan(backward_step, zero_row, outputs, reverse=True)
    return solved


def reference(source, coupling_x, coupling_y, reaction):
    halfway = sweep(source, coupling_x, reaction)
    turned = sweep(jnp.moveaxis(halfway, 1, 0), jnp.moveaxis(coupling_y, 1, 0), jnp.moveaxis(reaction, 1, 0))
    return jnp.moveaxis(turned, 0, 1)
```

```python
import functools

import jax
import jax.numpy as jnp
from jax import lax
from jax.experimental import pallas as pl
from jax.experimental.pallas import tpu as pltpu
from jax.sharding import PartitionSpec as P

MESH = pl.DeviceIdType.MESH
LONG = 128


def sweep(prev, slope, s, g):
    here = prev + slope
    if g is None:
        return here, slope + s * here
    return here, (slope - g) + s * here


def join_coefs(maps, long):
    one = jnp.ones_like(maps[0][0])
    zero = jnp.zeros_like(one)
    if long:
        ratio, out = zero, []
        for a, b, c, d in maps:
            inv = 1.0 / (c * ratio + d)
            nxt = (a * ratio + b) * inv
            out.append((ratio, inv, nxt))
            ratio = nxt
        return out, 1.0 / (1.0 + ratio)
    hu, hd, out = zero, one, []
    for a, b, c, d in maps:
        out.append((hu, hd))
        hu, hd = a * hu + b * hd, c * hu + d * hd
    return out, 1.0 / (hu + hd)


def join(maps, offs, coefs, long):
    steps, last = coefs
    zero = jnp.zeros_like(last)
    if long:
        sigma, sig = zero, []
        for (a, b, c, d), (p, q), (_, _, nxt) in zip(maps, offs, steps):
            sig.append(sigma)
            sigma = (a * sigma + p) - nxt * (c * sigma + q)
        slope, states = -sigma * last, []
        for k in reversed(range(len(maps))):
            ratio, inv, _ = steps[k]
            slope = (slope - (maps[k][2] * sig[k] + offs[k][1])) * inv
            states.append((ratio * slope + sig[k], slope))
        return states[::-1]
    u, s, part = zero, zero, []
    for (a, b, c, d), (p, q) in zip(maps, offs):
        part.append((u, s))
        u, s = (a * u + b * s) + p, (c * u + d * s) + q
    t = -(u + s) * last
    return [(pu + t * hu, ps + t * hd) for (pu, ps), (hu, hd) in zip(part, steps)]


def kernel(nx, ny, lx, ly, owners, f_ref, kx_ref, ky_ref, r_ref, out_ref,
           seg_s, seg_r, ent_s, ent_r, yc, yo, sy_v, g_v,
           seg_ss, seg_rs, ent_ss, ent_rs, yc_ss, yc_rs, yo_ss, yo_rs):
    gx, gy = lax.axis_index("gx"), lax.axis_index("gy")
    every = nx // owners
    rows = ly // owners
    mine = gx // every

    barrier = pltpu.get_barrier_semaphore()
    for k in range(1, nx):
        pl.semaphore_signal(barrier, inc=1, device_id=(lax.rem(gx + k, nx), gy), device_id_type=MESH)
    for k in range(1, ny):
        pl.semaphore_signal(barrier, inc=1, device_id=(gx, lax.rem(gy + k, ny)), device_id_type=MESH)

    one = jnp.ones((ly, f_ref.shape[1]), jnp.float32)
    zero = jnp.zeros_like(one)
    h1, h2, h3 = (one, zero), (zero, one), (zero, zero)
    cells = []
    for i in range(lx):
        at = pl.ds(i * ly, ly)
        inv = 1.0 / kx_ref[at, :]
        s, g = r_ref[at, :] * inv, f_ref[at, :] * inv
        h1, h2, h3 = sweep(*h1, s, None), sweep(*h2, s, None), sweep(*h3, s, g)
        cells.append((h1[0], h2[0], h3[0]))
    for v, val in enumerate((h1[0], h2[0], h1[1], h2[1], h3[0], h3[1])):
        for o in range(owners):
            seg_s[o, v] = val[o * rows:(o + 1) * rows, :]

    pl.semaphore_wait(barrier, nx - 1 + ny - 1)

    def seg_copy(o):
        return pltpu.make_async_remote_copy(
            src_ref=seg_s.at[o], dst_ref=seg_r.at[gx],
            send_sem=seg_ss.at[o], recv_sem=seg_rs.at[gx],
            device_id=(o * every, gy), device_id_type=MESH)

    for k in range(1, owners):
        seg_copy(lax.rem(mine + k, owners)).start()
    if every > 1:
        @pl.when(lax.rem(gx, every) != 0)
        def _():
            seg_copy(mine).start()

    ivals = []
    for i in range(lx):
        at = pl.ds(i * ly, ly)
        inv = 1.0 / ky_ref[at, :]
        ivals.append(inv)
        sy_v[at, :] = r_ref[at, :] * inv
    one8 = jnp.ones((lx, f_ref.shape[1]), jnp.float32)
    zero8 = jnp.zeros_like(one8)
    y1, y2, ycells, sy = (one8, zero8), (zero8, one8), [], []
    for j in range(ly):
        s = sy_v[pl.ds(j, lx, stride=ly), :]
        sy.append(s)
        y1, y2 = sweep(*y1, s, None), sweep(*y2, s, None)
        ycells.append((y1[0], y2[0]))
    for v, val in enumerate((y1[0], y2[0], y1[1], y2[1])):
        yc[gy, v] = val

    def y_copy(buf, ss, rs, k):
        to = lax.rem(gy + k, ny)
        return pltpu.make_async_remote_copy(
            src_ref=buf.at[gy], dst_ref=buf.at[gy],
            send_sem=ss.at[to], recv_sem=rs.at[gy],
            device_id=(gx, to), device_id_type=MESH)

    def y_arrived(buf, ss, rs, k):
        frm = lax.rem(gy + k, ny)
        pltpu.make_async_remote_copy(
            src_ref=buf.at[frm], dst_ref=buf.at[frm],
            send_sem=ss.at[frm], recv_sem=rs.at[frm],
            device_id=(gx, frm), device_id_type=MESH).wait_recv()

    for k in range(1, ny):
        y_copy(yc, yc_ss, yc_rs, k).start()

    def ent_copy(to):
        return pltpu.make_async_remote_copy(
            src_ref=ent_s.at[to], dst_ref=ent_r.at[mine],
            send_sem=ent_ss.at[to], recv_sem=ent_rs.at[mine],
            device_id=(to, gy), device_id_type=MESH)

    def own():
        seg_r[gx] = seg_s[mine]
        for k in range(1, nx):
            frm = lax.rem(gx + k, nx)
            pltpu.make_async_remote_copy(
                src_ref=seg_s.at[0], dst_ref=seg_r.at[frm],
                send_sem=seg_ss.at[0], recv_sem=seg_rs.at[frm],
                device_id=(frm, gy), device_id_type=MESH).wait_recv()
        maps = [tuple(seg_r[d, v] for v in range(4)) for d in range(nx)]
        offs = [tuple(seg_r[d, v] for v in (4, 5)) for d in range(nx)]
        long = nx * lx > LONG
        for d, (u, s) in enumerate(join(maps, offs, join_coefs(maps, long), long)):
            ent_s[d, 0] = u
            ent_s[d, 1] = s
        for k in range(1, nx):
            ent_copy(lax.rem(gx + k, nx)).start()
        ent_r[mine] = ent_s[gx]

    if every > 1:
        pl.when(lax.rem(gx, every) == 0)(own)
    else:
        own()

    for k in range(1, ny):
        y_arrived(yc, yc_ss, yc_rs, k)
    ymaps = [tuple(yc[d, v] for v in range(4)) for d in range(ny)]
    ylong = ny * ly > LONG
    ycoefs = join_coefs(ymaps, ylong)

    def ent_arrived(o):
        pltpu.make_async_remote_copy(
            src_ref=ent_s.at[0], dst_ref=ent_r.at[o],
            send_sem=ent_ss.at[0], recv_sem=ent_rs.at[o],
            device_id=(o * every, gy), device_id_type=MESH).wait_recv()

    for k in range(1, owners):
        ent_arrived(lax.rem(mine + k, owners))
    if every > 1:
        @pl.when(lax.rem(gx, every) != 0)
        def _():
            ent_arrived(mine)

    u0 = jnp.concatenate([ent_r[o, 0] for o in range(owners)], axis=0)
    s0 = jnp.concatenate([ent_r[o, 1] for o in range(owners)], axis=0)
    for i in range(lx):
        ca, cb, cg = cells[i]
        g_v[pl.ds(i * ly, ly), :] = ((ca * u0 + cb * s0) + cg) * ivals[i]

    y3, ygs = (zero8, zero8), []
    for j in range(ly):
        y3 = sweep(*y3, sy[j], g_v[pl.ds(j, lx, stride=ly), :])
        ygs.append(y3[0])
    yo[gy, 0] = y3[0]
    yo[gy, 1] = y3[1]
    for k in range(1, ny):
        y_copy(yo, yo_ss, yo_rs, k).start()
    for k in range(1, ny):
        y_arrived(yo, yo_ss, yo_rs, k)
    yoffs = [(yo[d, 0], yo[d, 1]) for d in range(ny)]
    u, s = zero8, zero8
    for d, (du, ds) in enumerate(join(ymaps, yoffs, ycoefs, ylong)):
        here = gy == d
        u, s = jnp.where(here, du, u), jnp.where(here, ds, s)
    for j in range(ly):
        ca, cb = ycells[j]
        out_ref[pl.ds(j, lx, stride=ly), :] = (ca * u + cb * s) + ygs[j]

    for k in range(1, owners):
        seg_copy(lax.rem(mine + k, owners)).wait_send()
    if every > 1:
        @pl.when(lax.rem(gx, every) != 0)
        def _():
            seg_copy(mine).wait_send()

    def own_sent():
        for k in range(1, nx):
            ent_copy(lax.rem(gx + k, nx)).wait_send()

    if every > 1:
        pl.when(lax.rem(gx, every) == 0)(own_sent)
    else:
        own_sent()
    for k in range(1, ny):
        y_copy(yc, yc_ss, yc_rs, k).wait_send()
        y_copy(yo, yo_ss, yo_rs, k).wait_send()


def solution(mesh):
    nx, ny = mesh.shape["gx"], mesh.shape["gy"]

    def per_device(source, coupling_x, coupling_y, reaction):
        lx, ly, nz = source.shape
        owners = min(nx, ly // 2)
        rows = ly // owners
        f32 = jnp.float32
        dma = pltpu.SemaphoreType.DMA
        vmem = pl.BlockSpec(memory_space=pltpu.VMEM)
        flat = [a.reshape(lx * ly, nz) for a in (source, coupling_x, coupling_y, reaction)]
        out = pl.pallas_call(
            functools.partial(kernel, nx, ny, lx, ly, owners),
            out_shape=jax.ShapeDtypeStruct((lx * ly, nz), f32),
            in_specs=[vmem] * 4,
            out_specs=vmem,
            scratch_shapes=[
                pltpu.VMEM((owners, 6, rows, nz), f32),
                pltpu.VMEM((nx, 6, rows, nz), f32),
                pltpu.VMEM((nx, 2, rows, nz), f32),
                pltpu.VMEM((owners, 2, rows, nz), f32),
                pltpu.VMEM((ny, 4, lx, nz), f32),
                pltpu.VMEM((ny, 2, lx, nz), f32),
                pltpu.VMEM((lx * ly, nz), f32),
                pltpu.VMEM((lx * ly, nz), f32),
                dma((owners,)), dma((nx,)), dma((nx,)), dma((owners,)),
                dma((ny,)), dma((ny,)), dma((ny,)), dma((ny,)),
            ],
            compiler_params=pltpu.CompilerParams(
                collective_id=0, has_side_effects=True, vmem_limit_bytes=8 * 1024 * 1024),
        )(*flat)
        return out.reshape(lx, ly, nz)

    spec = P("gx", "gy", None)
    return jax.shard_map(per_device, mesh=mesh, in_specs=(spec,) * 4, out_specs=spec, check_vma=False)
```

```python
import functools

import jax
import jax.numpy as jnp
from jax import lax
from jax.experimental import pallas as pl
from jax.experimental.pallas import tpu as pltpu
from jax.sharding import PartitionSpec as P

MESH = pl.DeviceIdType.MESH
LONG = 128


def sweep(prev, slope, s, g):
    here = prev + slope
    if g is None:
        return here, slope + s * here
    return here, (slope - g) + s * here


def join_coefs(maps, long):
    one = jnp.ones_like(maps[0][0])
    zero = jnp.zeros_like(one)
    if long:
        ratio, out = zero, []
        for a, b, c, d in maps:
            inv = 1.0 / (c * ratio + d)
            nxt = (a * ratio + b) * inv
            out.append((ratio, inv, nxt))
            ratio = nxt
        return out, 1.0 / (1.0 + ratio)
    hu, hd, out = zero, one, []
    for a, b, c, d in maps:
        out.append((hu, hd))
        hu, hd = a * hu + b * hd, c * hu + d * hd
    return out, 1.0 / (hu + hd)


def join(maps, offs, coefs, long):
    steps, last = coefs
    zero = jnp.zeros_like(last)
    if long:
        sigma, sig = zero, []
        for (a, b, c, d), (p, q), (_, _, nxt) in zip(maps, offs, steps):
            sig.append(sigma)
            sigma = (a * sigma + p) - nxt * (c * sigma + q)
        slope, states = -sigma * last, []
        for k in reversed(range(len(maps))):
            ratio, inv, _ = steps[k]
            slope = (slope - (maps[k][2] * sig[k] + offs[k][1])) * inv
            states.append((ratio * slope + sig[k], slope))
        return states[::-1]
    u, s, part = zero, zero, []
    for (a, b, c, d), (p, q) in zip(maps, offs):
        part.append((u, s))
        u, s = (a * u + b * s) + p, (c * u + d * s) + q
    t = -(u + s) * last
    return [(pu + t * hu, ps + t * hd) for (pu, ps), (hu, hd) in zip(part, steps)]


def kernel(nx, ny, lx, ly, owners, f_hbm, kx_hbm, ky_hbm, r_hbm, out_ref,
           f_ref, kx_ref, ky_ref, r_ref, load_sems, seg_s, seg_r, ent_s, ent_r, yc, yo, sy_v, g_v,
           seg_ss, seg_rs, ent_ss, ent_rs, yc_ss, yc_rs, yo_ss, yo_rs):
    gx, gy = lax.axis_index("gx"), lax.axis_index("gy")
    rows = ly // owners
    base = (nx - owners) // 2
    mine = lax.rem(gx + (nx - base), owners)
    is_owner = (gx >= base) & (gx < base + owners)
    far_first = sorted(range(1, owners), key=lambda k: abs(k - owners / 2))
    far_first_x = sorted(range(1, nx), key=lambda k: abs(k - nx / 2))

    barrier = pltpu.get_barrier_semaphore()
    for k in range(1, nx):
        pl.semaphore_signal(barrier, inc=1, device_id=(lax.rem(gx + k, nx), gy), device_id_type=MESH)
    for k in range(1, ny):
        pl.semaphore_signal(barrier, inc=1, device_id=(gx, lax.rem(gy + k, ny)), device_id_type=MESH)

    loads = [
        pltpu.make_async_copy(src, dst, load_sems.at[n])
        for n, (src, dst) in enumerate(
            ((kx_hbm, kx_ref), (r_hbm, r_ref), (f_hbm, f_ref), (ky_hbm, ky_ref)))
    ]
    for load in loads:
        load.start()
    for load in loads[:3]:
        load.wait()

    one = jnp.ones((ly, f_ref.shape[1]), jnp.float32)
    zero = jnp.zeros_like(one)
    h1, h2, h3 = (one, zero), (zero, one), (zero, zero)
    cells = []
    for i in range(lx):
        at = pl.ds(i * ly, ly)
        inv = 1.0 / kx_ref[at, :]
        s, g = r_ref[at, :] * inv, f_ref[at, :] * inv
        h1, h2, h3 = sweep(*h1, s, None), sweep(*h2, s, None), sweep(*h3, s, g)
        cells.append((h1[0], h2[0], h3[0]))
    for v, val in enumerate((h1[0], h2[0], h1[1], h2[1], h3[0], h3[1])):
        for o in range(owners):
            seg_s[o, v] = val[o * rows:(o + 1) * rows, :]

    pl.semaphore_wait(barrier, nx - 1 + ny - 1)

    def seg_copy(o):
        return pltpu.make_async_remote_copy(
            src_ref=seg_s.at[o], dst_ref=seg_r.at[gx],
            send_sem=seg_ss.at[o], recv_sem=seg_rs.at[gx],
            device_id=(base + o, gy), device_id_type=MESH)

    if owners < nx:
        @pl.when(jnp.logical_not(is_owner))
        def _():
            seg_copy(mine).start()
    for k in far_first:
        seg_copy(lax.rem(mine + k, owners)).start()

    loads[3].wait()

    ivals = []
    for i in range(lx):
        at = pl.ds(i * ly, ly)
        inv = 1.0 / ky_ref[at, :]
        ivals.append(inv)
        sy_v[at, :] = r_ref[at, :] * inv
    one8 = jnp.ones((lx, f_ref.shape[1]), jnp.float32)
    zero8 = jnp.zeros_like(one8)
    y1, y2, ycells, sy = (one8, zero8), (zero8, one8), [], []
    for j in range(ly):
        s = sy_v[pl.ds(j, lx, stride=ly), :]
        sy.append(s)
        y1, y2 = sweep(*y1, s, None), sweep(*y2, s, None)
        ycells.append((y1[0], y2[0]))
    for v, val in enumerate((y1[0], y2[0], y1[1], y2[1])):
        yc[gy, v] = val

    def y_copy(buf, ss, rs, k):
        to = lax.rem(gy + k, ny)
        return pltpu.make_async_remote_copy(
            src_ref=buf.at[gy], dst_ref=buf.at[gy],
            send_sem=ss.at[to], recv_sem=rs.at[gy],
            device_id=(gx, to), device_id_type=MESH)

    def y_arrived(buf, ss, rs, k):
        frm = lax.rem(gy + k, ny)
        pltpu.make_async_remote_copy(
            src_ref=buf.at[frm], dst_ref=buf.at[frm],
            send_sem=ss.at[frm], recv_sem=rs.at[frm],
            device_id=(gx, frm), device_id_type=MESH).wait_recv()

    for k in range(1, ny):
        y_copy(yc, yc_ss, yc_rs, k).start()

    def ent_copy(to):
        return pltpu.make_async_remote_copy(
            src_ref=ent_s.at[to], dst_ref=ent_r.at[mine],
            send_sem=ent_ss.at[to], recv_sem=ent_rs.at[mine],
            device_id=(to, gy), device_id_type=MESH)

    def own():
        seg_r[gx] = seg_s[mine]
        for k in range(1, nx):
            frm = lax.rem(gx + k, nx)
            pltpu.make_async_remote_copy(
                src_ref=seg_s.at[0], dst_ref=seg_r.at[frm],
                send_sem=seg_ss.at[0], recv_sem=seg_rs.at[frm],
                device_id=(frm, gy), device_id_type=MESH).wait_recv()
        maps = [tuple(seg_r[d, v] for v in range(4)) for d in range(nx)]
        offs = [tuple(seg_r[d, v] for v in (4, 5)) for d in range(nx)]
        long = nx * lx > LONG
        for d, (u, s) in enumerate(join(maps, offs, join_coefs(maps, long), long)):
            ent_s[d, 0] = u
            ent_s[d, 1] = s
        for k in far_first_x:
            ent_copy(lax.rem(gx + k, nx)).start()
        ent_r[mine] = ent_s[gx]

    if owners < nx:
        pl.when(is_owner)(own)
    else:
        own()

    for k in range(1, ny):
        y_arrived(yc, yc_ss, yc_rs, k)
    ymaps = [tuple(yc[d, v] for v in range(4)) for d in range(ny)]
    ylong = ny * ly > LONG
    ycoefs = join_coefs(ymaps, ylong)

    def ent_arrived(o):
        pltpu.make_async_remote_copy(
            src_ref=ent_s.at[0], dst_ref=ent_r.at[o],
            send_sem=ent_ss.at[0], recv_sem=ent_rs.at[o],
            device_id=(base + o, gy), device_id_type=MESH).wait_recv()

    for k in range(1, owners):
        ent_arrived(lax.rem(mine + k, owners))
    if owners < nx:
        @pl.when(jnp.logical_not(is_owner))
        def _():
            ent_arrived(mine)

    u0 = jnp.concatenate([ent_r[o, 0] for o in range(owners)], axis=0)
    s0 = jnp.concatenate([ent_r[o, 1] for o in range(owners)], axis=0)
    for i in range(lx):
        ca, cb, cg = cells[i]
        g_v[pl.ds(i * ly, ly), :] = ((ca * u0 + cb * s0) + cg) * ivals[i]

    y3, ygs = (zero8, zero8), []
    for j in range(ly):
        y3 = sweep(*y3, sy[j], g_v[pl.ds(j, lx, stride=ly), :])
        ygs.append(y3[0])
    yo[gy, 0] = y3[0]
    yo[gy, 1] = y3[1]
    for k in range(1, ny):
        y_copy(yo, yo_ss, yo_rs, k).start()
    for k in range(1, ny):
        y_arrived(yo, yo_ss, yo_rs, k)
    yoffs = [(yo[d, 0], yo[d, 1]) for d in range(ny)]
    u, s = zero8, zero8
    for d, (du, ds) in enumerate(join(ymaps, yoffs, ycoefs, ylong)):
        here = gy == d
        u, s = jnp.where(here, du, u), jnp.where(here, ds, s)
    for j in range(ly):
        ca, cb = ycells[j]
        out_ref[pl.ds(j, lx, stride=ly), :] = (ca * u + cb * s) + ygs[j]

    for k in range(1, owners):
        seg_copy(lax.rem(mine + k, owners)).wait_send()
    if owners < nx:
        @pl.when(jnp.logical_not(is_owner))
        def _():
            seg_copy(mine).wait_send()

    def own_sent():
        for k in range(1, nx):
            ent_copy(lax.rem(gx + k, nx)).wait_send()

    if owners < nx:
        pl.when(is_owner)(own_sent)
    else:
        own_sent()
    for k in range(1, ny):
        y_copy(yc, yc_ss, yc_rs, k).wait_send()
        y_copy(yo, yo_ss, yo_rs, k).wait_send()


def solution(mesh):
    nx, ny = mesh.shape["gx"], mesh.shape["gy"]

    def per_device(source, coupling_x, coupling_y, reaction):
        lx, ly, nz = source.shape
        owners = min(nx, ly // 4)
        rows = ly // owners
        f32 = jnp.float32
        dma = pltpu.SemaphoreType.DMA
        vmem = pl.BlockSpec(memory_space=pltpu.VMEM)
        flat = [
            pltpu.with_memory_space_constraint(a.reshape(lx * ly, nz), pltpu.HBM)
            for a in (source, coupling_x, coupling_y, reaction)
        ]
        out = pl.pallas_call(
            functools.partial(kernel, nx, ny, lx, ly, owners),
            out_shape=jax.ShapeDtypeStruct((lx * ly, nz), f32),
            in_specs=[pl.BlockSpec(memory_space=pltpu.HBM)] * 4,
            out_specs=vmem,
            scratch_shapes=[
                *[pltpu.VMEM((lx * ly, nz), f32)] * 4, dma((4,)),
                pltpu.VMEM((owners, 6, rows, nz), f32),
                pltpu.VMEM((nx, 6, rows, nz), f32),
                pltpu.VMEM((nx, 2, rows, nz), f32),
                pltpu.VMEM((owners, 2, rows, nz), f32),
                pltpu.VMEM((ny, 4, lx, nz), f32),
                pltpu.VMEM((ny, 2, lx, nz), f32),
                pltpu.VMEM((lx * ly, nz), f32),
                pltpu.VMEM((lx * ly, nz), f32),
                dma((owners,)), dma((nx,)), dma((nx,)), dma((owners,)),
                dma((ny,)), dma((ny,)), dma((ny,)), dma((ny,)),
            ],
            compiler_params=pltpu.CompilerParams(
                collective_id=0, has_side_effects=True, vmem_limit_bytes=16 * 1024 * 1024),
        )(*flat)
        return out.reshape(lx, ly, nz)

    spec = P("gx", "gy", None)
    return jax.shard_map(per_device, mesh=mesh, in_specs=(spec,) * 4, out_specs=spec, check_vma=False)
```

```python
import functools

import jax
import jax.numpy as jnp
from jax import lax
from jax.experimental import pallas as pl
from jax.experimental.pallas import tpu as pltpu
from jax.sharding import PartitionSpec as P

MESH = pl.DeviceIdType.MESH
LONG = 128


def sweep(prev, slope, s, g):
    here = prev + slope
    if g is None:
        return here, slope + s * here
    return here, (slope - g) + s * here


def join_coefs(maps, long):
    one = jnp.ones_like(maps[0][0])
    zero = jnp.zeros_like(one)
    if long:
        ratio, out = zero, []
        for a, b, c, d in maps:
            inv = 1.0 / (c * ratio + d)
            nxt = (a * ratio + b) * inv
            out.append((ratio, inv, nxt))
            ratio = nxt
        return out, 1.0 / (1.0 + ratio)
    hu, hd, out = zero, one, []
    for a, b, c, d in maps:
        out.append((hu, hd))
        hu, hd = a * hu + b * hd, c * hu + d * hd
    return out, 1.0 / (hu + hd)


def join(maps, offs, coefs, long):
    steps, last = coefs
    zero = jnp.zeros_like(last)
    if long:
        sigma, sig = zero, []
        for (a, b, c, d), (p, q), (_, _, nxt) in zip(maps, offs, steps):
            sig.append(sigma)
            sigma = (a * sigma + p) - nxt * (c * sigma + q)
        slope, states = -sigma * last, []
        for k in reversed(range(len(maps))):
            ratio, inv, _ = steps[k]
            slope = (slope - (maps[k][2] * sig[k] + offs[k][1])) * inv
            states.append((ratio * slope + sig[k], slope))
        return states[::-1]
    u, s, part = zero, zero, []
    for (a, b, c, d), (p, q) in zip(maps, offs):
        part.append((u, s))
        u, s = (a * u + b * s) + p, (c * u + d * s) + q
    t = -(u + s) * last
    return [(pu + t * hu, ps + t * hd) for (pu, ps), (hu, hd) in zip(part, steps)]


def kernel(nx, ny, lx, ly, owners, f_hbm, kx_hbm, ky_hbm, r_hbm, out_ref,
           f_ref, kx_ref, ky_ref, r_ref, load_sems, seg_s, seg_r, ent_s, ent_r, yc, yo, sy_v, g_v,
           seg_ss, seg_rs, ent_ss, ent_rs, yc_ss, yc_rs, yo_ss, yo_rs):
    gx, gy = lax.axis_index("gx"), lax.axis_index("gy")
    rows = ly // owners
    base = (nx - owners) // 2
    mine = lax.rem(gx + (nx - base), owners)
    is_owner = (gx >= base) & (gx < base + owners)
    far_first = sorted(range(1, owners), key=lambda k: abs(k - owners / 2))
    far_first_x = sorted(range(1, nx), key=lambda k: abs(k - nx / 2))

    barrier = pltpu.get_barrier_semaphore()

    @pl.when(is_owner)
    def _():
        for k in far_first_x:
            pl.semaphore_signal(barrier, inc=1, device_id=(lax.rem(gx + k, nx), gy), device_id_type=MESH)

    loads = [
        pltpu.make_async_copy(src, dst, load_sems.at[n])
        for n, (src, dst) in enumerate(
            ((kx_hbm, kx_ref), (r_hbm, r_ref), (f_hbm, f_ref), (ky_hbm, ky_ref)))
    ]
    for load in loads:
        load.start()
    for k in range(1, ny):
        pl.semaphore_signal(barrier, inc=1, device_id=(gx, lax.rem(gy + k, ny)), device_id_type=MESH)
    for load in loads[:3]:
        load.wait()

    one = jnp.ones((ly, f_ref.shape[1]), jnp.float32)
    zero = jnp.zeros_like(one)
    h1, h2, h3 = (one, zero), (zero, one), (zero, zero)
    cells = []
    for i in range(lx):
        at = pl.ds(i * ly, ly)
        inv = 1.0 / kx_ref[at, :]
        s, g = r_ref[at, :] * inv, f_ref[at, :] * inv
        h1, h2, h3 = sweep(*h1, s, None), sweep(*h2, s, None), sweep(*h3, s, g)
        cells.append((h1[0], h2[0], h3[0]))
    for v, val in enumerate((h1[0], h2[0], h1[1], h3[0], h3[1])):
        for o in range(owners):
            seg_s[o, v] = val[o * rows:(o + 1) * rows, :]

    pl.semaphore_wait(barrier, owners + ny - 1 - is_owner.astype(jnp.int32))

    def seg_copy(o):
        return pltpu.make_async_remote_copy(
            src_ref=seg_s.at[o], dst_ref=seg_r.at[gx],
            send_sem=seg_ss.at[o], recv_sem=seg_rs.at[gx],
            device_id=(base + o, gy), device_id_type=MESH)

    if owners < nx:
        @pl.when(jnp.logical_not(is_owner))
        def _():
            seg_copy(mine).start()
    for k in far_first:
        seg_copy(lax.rem(mine + k, owners)).start()

    loads[3].wait()

    ivals = []
    for i in range(lx):
        at = pl.ds(i * ly, ly)
        inv = 1.0 / ky_ref[at, :]
        ivals.append(inv)
        sy_v[at, :] = r_ref[at, :] * inv
    one8 = jnp.ones((lx, f_ref.shape[1]), jnp.float32)
    zero8 = jnp.zeros_like(one8)
    y1, y2, ycells, sy = (one8, zero8), (zero8, one8), [], []
    for j in range(ly):
        s = sy_v[pl.ds(j, lx, stride=ly), :]
        sy.append(s)
        y1, y2 = sweep(*y1, s, None), sweep(*y2, s, None)
        ycells.append((y1[0], y2[0]))
    for v, val in enumerate((y1[0], y2[0], y1[1], y2[1])):
        yc[gy, v] = val

    def y_copy(buf, ss, rs, k):
        to = lax.rem(gy + k, ny)
        return pltpu.make_async_remote_copy(
            src_ref=buf.at[gy], dst_ref=buf.at[gy],
            send_sem=ss.at[to], recv_sem=rs.at[gy],
            device_id=(gx, to), device_id_type=MESH)

    def y_arrived(buf, ss, rs, k):
        frm = lax.rem(gy + k, ny)
        pltpu.make_async_remote_copy(
            src_ref=buf.at[frm], dst_ref=buf.at[frm],
            send_sem=ss.at[frm], recv_sem=rs.at[frm],
            device_id=(gx, frm), device_id_type=MESH).wait_recv()

    for k in range(1, ny):
        y_copy(yc, yc_ss, yc_rs, k).start()

    def ent_copy(to):
        return pltpu.make_async_remote_copy(
            src_ref=ent_s.at[to], dst_ref=ent_r.at[mine],
            send_sem=ent_ss.at[to], recv_sem=ent_rs.at[mine],
            device_id=(to, gy), device_id_type=MESH)

    def own():
        seg_r[gx] = seg_s[mine]
        for k in range(1, nx):
            frm = lax.rem(gx + k, nx)
            pltpu.make_async_remote_copy(
                src_ref=seg_s.at[0], dst_ref=seg_r.at[frm],
                send_sem=seg_ss.at[0], recv_sem=seg_rs.at[frm],
                device_id=(frm, gy), device_id_type=MESH).wait_recv()
        maps = []
        for d in range(nx):
            a, b, c = (seg_r[d, v] for v in range(3))
            maps.append((a, b, c, (1.0 + b * c) / a))
        offs = [(seg_r[d, 3], seg_r[d, 4]) for d in range(nx)]
        long = nx * lx > LONG
        for d, (u, s) in enumerate(join(maps, offs, join_coefs(maps, long), long)):
            ent_s[d, 0] = u
            ent_s[d, 1] = s
        for k in far_first_x:
            ent_copy(lax.rem(gx + k, nx)).start()
        ent_r[mine] = ent_s[gx]

    if owners < nx:
        pl.when(is_owner)(own)
    else:
        own()

    for k in range(1, ny):
        y_arrived(yc, yc_ss, yc_rs, k)
    ymaps = [tuple(yc[d, v] for v in range(4)) for d in range(ny)]
    ylong = ny * ly > LONG
    ycoefs = join_coefs(ymaps, ylong)

    def ent_arrived(o):
        pltpu.make_async_remote_copy(
            src_ref=ent_s.at[0], dst_ref=ent_r.at[o],
            send_sem=ent_ss.at[0], recv_sem=ent_rs.at[o],
            device_id=(base + o, gy), device_id_type=MESH).wait_recv()

    for k in range(1, owners):
        ent_arrived(lax.rem(mine + k, owners))
    if owners < nx:
        @pl.when(jnp.logical_not(is_owner))
        def _():
            ent_arrived(mine)

    u0 = jnp.concatenate([ent_r[o, 0] for o in range(owners)], axis=0)
    s0 = jnp.concatenate([ent_r[o, 1] for o in range(owners)], axis=0)
    for i in range(lx):
        ca, cb, cg = cells[i]
        g_v[pl.ds(i * ly, ly), :] = ((ca * u0 + cb * s0) + cg) * ivals[i]

    y3, ygs = (zero8, zero8), []
    for j in range(ly):
        y3 = sweep(*y3, sy[j], g_v[pl.ds(j, lx, stride=ly), :])
        ygs.append(y3[0])
    yo[gy, 0] = y3[0]
    yo[gy, 1] = y3[1]
    for k in range(1, ny):
        y_copy(yo, yo_ss, yo_rs, k).start()
    for k in range(1, ny):
        y_arrived(yo, yo_ss, yo_rs, k)
    yoffs = [(yo[d, 0], yo[d, 1]) for d in range(ny)]
    u, s = zero8, zero8
    for d, (du, ds) in enumerate(join(ymaps, yoffs, ycoefs, ylong)):
        here = gy == d
        u, s = jnp.where(here, du, u), jnp.where(here, ds, s)
    for j in range(ly):
        ca, cb = ycells[j]
        out_ref[pl.ds(j, lx, stride=ly), :] = (ca * u + cb * s) + ygs[j]

    for k in range(1, owners):
        seg_copy(lax.rem(mine + k, owners)).wait_send()
    if owners < nx:
        @pl.when(jnp.logical_not(is_owner))
        def _():
            seg_copy(mine).wait_send()

    def own_sent():
        for k in range(1, nx):
            ent_copy(lax.rem(gx + k, nx)).wait_send()

    if owners < nx:
        pl.when(is_owner)(own_sent)
    else:
        own_sent()
    for k in range(1, ny):
        y_copy(yc, yc_ss, yc_rs, k).wait_send()
        y_copy(yo, yo_ss, yo_rs, k).wait_send()


def solution(mesh):
    nx, ny = mesh.shape["gx"], mesh.shape["gy"]

    def per_device(source, coupling_x, coupling_y, reaction):
        lx, ly, nz = source.shape
        owners = min(nx, ly // 8)
        rows = ly // owners
        f32 = jnp.float32
        dma = pltpu.SemaphoreType.DMA
        vmem = pl.BlockSpec(memory_space=pltpu.VMEM)
        flat = [
            pltpu.with_memory_space_constraint(a.reshape(lx * ly, nz), pltpu.HBM)
            for a in (source, coupling_x, coupling_y, reaction)
        ]
        out = pl.pallas_call(
            functools.partial(kernel, nx, ny, lx, ly, owners),
            out_shape=jax.ShapeDtypeStruct((lx * ly, nz), f32),
            in_specs=[pl.BlockSpec(memory_space=pltpu.HBM)] * 4,
            out_specs=vmem,
            scratch_shapes=[
                *[pltpu.VMEM((lx * ly, nz), f32)] * 4, dma((4,)),
                pltpu.VMEM((owners, 5, rows, nz), f32),
                pltpu.VMEM((nx, 5, rows, nz), f32),
                pltpu.VMEM((nx, 2, rows, nz), f32),
                pltpu.VMEM((owners, 2, rows, nz), f32),
                pltpu.VMEM((ny, 4, lx, nz), f32),
                pltpu.VMEM((ny, 2, lx, nz), f32),
                pltpu.VMEM((lx * ly, nz), f32),
                pltpu.VMEM((lx * ly, nz), f32),
                dma((owners,)), dma((nx,)), dma((nx,)), dma((owners,)),
                dma((ny,)), dma((ny,)), dma((ny,)), dma((ny,)),
            ],
            compiler_params=pltpu.CompilerParams(
                collective_id=0, has_side_effects=True, vmem_limit_bytes=16 * 1024 * 1024),
        )(*flat)
        return out.reshape(lx, ly, nz)

    spec = P("gx", "gy", None)
    return jax.shard_map(per_device, mesh=mesh, in_specs=(spec,) * 4, out_specs=spec, check_vma=False)
```

```python
import functools

import jax
import jax.numpy as jnp
from jax import lax
from jax.experimental import pallas as pl
from jax.experimental.pallas import tpu as pltpu
from jax.sharding import PartitionSpec as P

MESH = pl.DeviceIdType.MESH
LONG = 128


def sweep(prev, slope, s, g):
    here = prev + slope
    if g is None:
        return here, slope + s * here
    return here, (slope - g) + s * here


def join_coefs(maps, long):
    one = jnp.ones_like(maps[0][0])
    zero = jnp.zeros_like(one)
    if long:
        ratio, out = zero, []
        for a, b, c, d in maps:
            inv = 1.0 / (c * ratio + d)
            nxt = (a * ratio + b) * inv
            out.append((ratio, inv, nxt))
            ratio = nxt
        return out, 1.0 / (1.0 + ratio)
    hu, hd, out = zero, one, []
    for a, b, c, d in maps:
        out.append((hu, hd))
        hu, hd = a * hu + b * hd, c * hu + d * hd
    return out, 1.0 / (hu + hd)


def join(maps, offs, coefs, long):
    steps, last = coefs
    zero = jnp.zeros_like(last)
    if long:
        sigma, sig = zero, []
        for (a, b, c, d), (p, q), (_, _, nxt) in zip(maps, offs, steps):
            sig.append(sigma)
            sigma = (a * sigma + p) - nxt * (c * sigma + q)
        slope, states = -sigma * last, []
        for k in reversed(range(len(maps))):
            ratio, inv, _ = steps[k]
            slope = (slope - (maps[k][2] * sig[k] + offs[k][1])) * inv
            states.append((ratio * slope + sig[k], slope))
        return states[::-1]
    u, s, part = zero, zero, []
    for (a, b, c, d), (p, q) in zip(maps, offs):
        part.append((u, s))
        u, s = (a * u + b * s) + p, (c * u + d * s) + q
    t = -(u + s) * last
    return [(pu + t * hu, ps + t * hd) for (pu, ps), (hu, hd) in zip(part, steps)]


def total(terms):
    while len(terms) > 1:
        terms = [sum(terms[k + 1:k + 2], terms[k]) for k in range(0, len(terms), 2)]
    return terms[0]


def kernel(nx, ny, lx, ly, owners, f_hbm, kx_hbm, ky_hbm, r_hbm, out_ref,
           f_ref, kx_ref, ky_ref, r_ref, load_sems, seg_s, seg_r, ent_s, ent_r, yc, yo, sy_v, fa_v, fb_v, fc_v,
           seg_ss, seg_rs, ent_ss, ent_rs, yc_ss, yc_rs, yo_ss, yo_rs):
    gx, gy = lax.axis_index("gx"), lax.axis_index("gy")
    rows = ly // owners
    base = (nx - owners) // 2
    mine = lax.rem(gx + (nx - base), owners)
    is_owner = (gx >= base) & (gx < base + owners)

    def elsewhere(d, act):
        if base <= d < base + owners:
            pl.when(gx != d)(lambda: act() and None)
        else:
            act()

    barrier = pltpu.get_barrier_semaphore()

    @pl.when(is_owner)
    def _():
        for k in range(1, nx):
            pl.semaphore_signal(barrier, inc=1, device_id=(lax.rem(gx + k, nx), gy), device_id_type=MESH)

    loads = [
        pltpu.make_async_copy(src, dst, load_sems.at[n])
        for n, (src, dst) in enumerate(
            ((kx_hbm, kx_ref), (r_hbm, r_ref), (f_hbm, f_ref), (ky_hbm, ky_ref)))
    ]
    for load in loads:
        load.start()
    for k in range(1, ny):
        pl.semaphore_signal(barrier, inc=1, device_id=(gx, lax.rem(gy + k, ny)), device_id_type=MESH)
    for load in loads[:3]:
        load.wait()

    one = jnp.ones((ly, f_ref.shape[1]), jnp.float32)
    zero = jnp.zeros_like(one)
    h1, h2, h3 = (one, zero), (zero, one), (zero, zero)
    cells = []
    for i in range(lx):
        at = pl.ds(i * ly, ly)
        inv = 1.0 / kx_ref[at, :]
        s, g = r_ref[at, :] * inv, f_ref[at, :] * inv
        h1, h2, h3 = sweep(*h1, s, None), sweep(*h2, s, None), sweep(*h3, s, g)
        cells.append((h1[0], h2[0], h3[0]))
    for v, val in enumerate((h1[0], h2[0], h1[1], h3[0], h3[1])):
        for o in range(owners):
            seg_s[o, v] = val[o * rows:(o + 1) * rows, :]

    pl.semaphore_wait(barrier, owners + ny - 1 - is_owner.astype(jnp.int32))

    def seg_copy(o):
        return pltpu.make_async_remote_copy(
            src_ref=seg_s.at[o], dst_ref=seg_r.at[gx],
            send_sem=seg_ss.at[o], recv_sem=seg_rs.at[gx],
            device_id=(base + o, gy), device_id_type=MESH)

    for o in range(owners):
        elsewhere(base + o, seg_copy(o).start)

    loads[3].wait()

    ivals = []
    for i in range(lx):
        at = pl.ds(i * ly, ly)
        inv = 1.0 / ky_ref[at, :]
        ivals.append(inv)
        sy_v[at, :] = r_ref[at, :] * inv
    one8 = jnp.ones((lx, f_ref.shape[1]), jnp.float32)
    zero8 = jnp.zeros_like(one8)
    y1, y2, ycells, sy = (one8, zero8), (zero8, one8), [], []
    for j in range(ly):
        s = sy_v[pl.ds(j, lx, stride=ly), :]
        sy.append(s)
        y1, y2 = sweep(*y1, s, None), sweep(*y2, s, None)
        ycells.append((y1[0], y2[0]))
    for v, val in enumerate((y1[0], y2[0], y1[1], y2[1])):
        yc[gy, v] = val

    def y_copy(buf, ss, rs, to):
        return pltpu.make_async_remote_copy(
            src_ref=buf.at[gy], dst_ref=buf.at[gy],
            send_sem=ss.at[to], recv_sem=rs.at[gy],
            device_id=(gx, to), device_id_type=MESH)

    def y_all(buf, ss, rs, act):
        for d in range(ny):
            @pl.when(gy != d)
            def _():
                getattr(y_copy(buf, ss, rs, d), act)()

    def y_arrived(buf, ss, rs):
        for d in range(ny):
            @pl.when(gy != d)
            def _():
                pltpu.make_async_remote_copy(
                    src_ref=buf.at[d], dst_ref=buf.at[d],
                    send_sem=ss.at[d], recv_sem=rs.at[d],
                    device_id=(gx, d), device_id_type=MESH).wait_recv()

    y_all(yc, yc_ss, yc_rs, "start")

    def ent_copy(to):
        return pltpu.make_async_remote_copy(
            src_ref=ent_s.at[to], dst_ref=ent_r.at[mine],
            send_sem=ent_ss.at[to], recv_sem=ent_rs.at[mine],
            device_id=(to, gy), device_id_type=MESH)

    def own():
        seg_r[gx] = seg_s[mine]
        for d in range(nx):
            elsewhere(d, pltpu.make_async_remote_copy(
                src_ref=seg_s.at[0], dst_ref=seg_r.at[d],
                send_sem=seg_ss.at[0], recv_sem=seg_rs.at[d],
                device_id=(d, gy), device_id_type=MESH).wait_recv)
        maps = []
        for d in range(nx):
            a, b, c = (seg_r[d, v] for v in range(3))
            maps.append((a, b, c, (1.0 + b * c) / a))
        offs = [(seg_r[d, 3], seg_r[d, 4]) for d in range(nx)]
        long = nx * lx > LONG
        for d, (u, s) in enumerate(join(maps, offs, join_coefs(maps, long), long)):
            ent_s[d, 0] = u
            ent_s[d, 1] = s
            elsewhere(d, ent_copy(d).start)
        ent_r[mine] = ent_s[gx]

    if owners < nx:
        pl.when(is_owner)(own)
    else:
        own()

    y_arrived(yc, yc_ss, yc_rs)
    ymaps = [tuple(yc[d, v] for v in range(4)) for d in range(ny)]
    ylong = ny * ly > LONG
    ycoefs = join_coefs(ymaps, ylong)

    for i, val in enumerate(cells):
        for buf, part in zip((fa_v, fb_v, fc_v), val):
            buf[pl.ds(i * ly, ly), :] = part * ivals[i]
    turned = [
        tuple(buf[pl.ds(j, lx, stride=ly), :] for buf in (fa_v, fb_v, fc_v)) for j in range(ly)
    ]
    up, us, qp, qs, weights = one8, zero8, zero8, one8, []
    for j in reversed(range(ly)):
        weights.append((us, qs))
        up, qp = up + sy[j] * us, qp + sy[j] * qs
        us, qs = us + up, qs + qp
    weights = weights[::-1]

    for o in range(owners):
        elsewhere(base + o, pltpu.make_async_remote_copy(
            src_ref=ent_s.at[0], dst_ref=ent_r.at[o],
            send_sem=ent_ss.at[0], recv_sem=ent_rs.at[o],
            device_id=(base + o, gy), device_id_type=MESH).wait_recv)

    g_y = []
    for j in range(ly):
        o, row = j // rows, pl.ds(j % rows, 1)
        fa, fb, fc = turned[j]
        g_y.append((fa * ent_r[o, 0, row, :] + fb * ent_r[o, 1, row, :]) + fc)
    yo[gy, 0] = -total([w[0] * g for w, g in zip(weights, g_y)])
    yo[gy, 1] = -total([w[1] * g for w, g in zip(weights, g_y)])
    y_all(yo, yo_ss, yo_rs, "start")
    y3, ygs = (zero8, zero8), []
    for j in range(ly):
        y3 = sweep(*y3, sy[j], g_y[j])
        ygs.append(y3[0])
    y_arrived(yo, yo_ss, yo_rs)
    yoffs = [(yo[d, 0], yo[d, 1]) for d in range(ny)]
    u, s = zero8, zero8
    for d, (du, ds) in enumerate(join(ymaps, yoffs, ycoefs, ylong)):
        here = gy == d
        u, s = jnp.where(here, du, u), jnp.where(here, ds, s)
    for j in range(ly):
        ca, cb = ycells[j]
        out_ref[pl.ds(j, lx, stride=ly), :] = (ca * u + cb * s) + ygs[j]

    for o in range(owners):
        elsewhere(base + o, seg_copy(o).wait_send)

    def own_sent():
        for d in range(nx):
            elsewhere(d, ent_copy(d).wait_send)

    if owners < nx:
        pl.when(is_owner)(own_sent)
    else:
        own_sent()
    y_all(yc, yc_ss, yc_rs, "wait_send")
    y_all(yo, yo_ss, yo_rs, "wait_send")


def solution(mesh):
    nx, ny = mesh.shape["gx"], mesh.shape["gy"]

    def per_device(source, coupling_x, coupling_y, reaction):
        lx, ly, nz = source.shape
        owners = min(nx, ly // 8)
        rows = ly // owners
        f32 = jnp.float32
        dma = pltpu.SemaphoreType.DMA
        vmem = pl.BlockSpec(memory_space=pltpu.VMEM)
        flat = [
            pltpu.with_memory_space_constraint(a.reshape(lx * ly, nz), pltpu.HBM)
            for a in (source, coupling_x, coupling_y, reaction)
        ]
        out = pl.pallas_call(
            functools.partial(kernel, nx, ny, lx, ly, owners),
            out_shape=jax.ShapeDtypeStruct((lx * ly, nz), f32),
            in_specs=[pl.BlockSpec(memory_space=pltpu.HBM)] * 4,
            out_specs=vmem,
            scratch_shapes=[
                *[pltpu.VMEM((lx * ly, nz), f32)] * 4, dma((4,)),
                pltpu.VMEM((owners, 5, rows, nz), f32),
                pltpu.VMEM((nx, 5, rows, nz), f32),
                pltpu.VMEM((nx, 2, rows, nz), f32),
                pltpu.VMEM((owners, 2, rows, nz), f32),
                pltpu.VMEM((ny, 4, lx, nz), f32),
                pltpu.VMEM((ny, 2, lx, nz), f32),
                *[pltpu.VMEM((lx * ly, nz), f32)] * 4,
                dma((owners,)), dma((nx,)), dma((nx,)), dma((owners,)),
                dma((ny,)), dma((ny,)), dma((ny,)), dma((ny,)),
            ],
            compiler_params=pltpu.CompilerParams(
                collective_id=0, has_side_effects=True, vmem_limit_bytes=16 * 1024 * 1024),
        )(*flat)
        return out.reshape(lx, ly, nz)

    spec = P("gx", "gy", None)
    return jax.shard_map(per_device, mesh=mesh, in_specs=(spec,) * 4, out_specs=spec, check_vma=False)
```

```python
import functools

import jax
import jax.numpy as jnp
from jax import lax
from jax.experimental import pallas as pl
from jax.experimental.pallas import tpu as pltpu
from jax.sharding import PartitionSpec as P

MESH = pl.DeviceIdType.MESH
LONG = 128


def sweep(prev, slope, s, g):
    here = prev + slope
    if g is None:
        return here, slope + s * here
    return here, (slope - g) + s * here


def join_coefs(maps, long):
    one = jnp.ones_like(maps[0][0])
    zero = jnp.zeros_like(one)
    if long:
        ratio, out = zero, []
        for a, b, c, d in maps:
            inv = 1.0 / (c * ratio + d)
            nxt = (a * ratio + b) * inv
            out.append((ratio, inv, nxt))
            ratio = nxt
        return out, 1.0 / (1.0 + ratio)
    hu, hd, out = zero, one, []
    for a, b, c, d in maps:
        out.append((hu, hd))
        hu, hd = a * hu + b * hd, c * hu + d * hd
    return out, 1.0 / (hu + hd)


def join(maps, offs, coefs, long):
    steps, last = coefs
    zero = jnp.zeros_like(last)
    if long:
        sigma, sig = zero, []
        for (a, b, c, d), (p, q), (_, _, nxt) in zip(maps, offs, steps):
            sig.append(sigma)
            sigma = (a * sigma + p) - nxt * (c * sigma + q)
        slope, states = -sigma * last, []
        for k in reversed(range(len(maps))):
            ratio, inv, _ = steps[k]
            slope = (slope - (maps[k][2] * sig[k] + offs[k][1])) * inv
            states.append((ratio * slope + sig[k], slope))
        return states[::-1]
    u, s, part = zero, zero, []
    for (a, b, c, d), (p, q) in zip(maps, offs):
        part.append((u, s))
        u, s = (a * u + b * s) + p, (c * u + d * s) + q
    t = -(u + s) * last
    return [(pu + t * hu, ps + t * hd) for (pu, ps), (hu, hd) in zip(part, steps)]


def total(terms):
    while len(terms) > 1:
        terms = [sum(terms[k + 1:k + 2], terms[k]) for k in range(0, len(terms), 2)]
    return terms[0]


def kernel(nx, ny, lx, ly, groups, f_hbm, kx_hbm, ky_hbm, r_hbm, out_ref,
           f_ref, kx_ref, ky_ref, r_ref, load_sems, seg_s, seg_r, ent_s, ent_r, yc, yo, sy_v, fa_v, fb_v, fc_v,
           seg_ss, seg_rs, ent_ss, ent_rs, yc_ss, yc_rs, yo_ss, yo_rs):
    gx, gy = lax.axis_index("gx"), lax.axis_index("gy")
    rows, half, owners = ly // groups, nx // 2, 2 * groups
    base = half - groups
    upper = (gx >= half).astype(jnp.int32)
    first = upper * half
    server = base + upper * groups
    mine = lax.rem(gx + (nx * groups - base), groups)
    is_owner = (gx >= base) & (gx < base + owners)

    def elsewhere(d, act):
        if base <= d < base + owners:
            pl.when(gx != d)(lambda: act() and None)
        else:
            act()

    barrier = pltpu.get_barrier_semaphore()

    @pl.when(is_owner)
    def _():
        for k in range(1, nx):
            pl.semaphore_signal(barrier, inc=1, device_id=(lax.rem(gx + k, nx), gy), device_id_type=MESH)

    loads = [
        pltpu.make_async_copy(src, dst, load_sems.at[n])
        for n, (src, dst) in enumerate(
            ((kx_hbm, kx_ref), (r_hbm, r_ref), (f_hbm, f_ref), (ky_hbm, ky_ref)))
    ]
    for load in loads:
        load.start()
    for k in range(1, ny):
        pl.semaphore_signal(barrier, inc=1, device_id=(gx, lax.rem(gy + k, ny)), device_id_type=MESH)
    for load in loads[:3]:
        load.wait()

    one = jnp.ones((ly, f_ref.shape[1]), jnp.float32)
    zero = jnp.zeros_like(one)
    h1, h2, h3 = (one, zero), (zero, one), (zero, zero)
    cells = []
    for i in range(lx):
        at = pl.ds(i * ly, ly)
        inv = 1.0 / kx_ref[at, :]
        s, g = r_ref[at, :] * inv, f_ref[at, :] * inv
        h1, h2, h3 = sweep(*h1, s, None), sweep(*h2, s, None), sweep(*h3, s, g)
        cells.append((h1[0], h2[0], h3[0]))
    for v, val in enumerate((h1[0], h2[0], h1[1], h3[0], h3[1])):
        for o in range(groups):
            seg_s[o, v] = val[o * rows:(o + 1) * rows, :]

    pl.semaphore_wait(barrier, owners + ny - 1 - is_owner.astype(jnp.int32))

    def seg_copy(o):
        return pltpu.make_async_remote_copy(
            src_ref=seg_s.at[o % groups], dst_ref=seg_r.at[gx],
            send_sem=seg_ss.at[o], recv_sem=seg_rs.at[gx],
            device_id=(base + o, gy), device_id_type=MESH)

    for o in range(owners):
        elsewhere(base + o, seg_copy(o).start)

    loads[3].wait()

    ivals = []
    for i in range(lx):
        at = pl.ds(i * ly, ly)
        inv = 1.0 / ky_ref[at, :]
        ivals.append(inv)
        sy_v[at, :] = r_ref[at, :] * inv
    one8 = jnp.ones((lx, f_ref.shape[1]), jnp.float32)
    zero8 = jnp.zeros_like(one8)
    y1, y2, ycells, sy = (one8, zero8), (zero8, one8), [], []
    for j in range(ly):
        s = sy_v[pl.ds(j, lx, stride=ly), :]
        sy.append(s)
        y1, y2 = sweep(*y1, s, None), sweep(*y2, s, None)
        ycells.append((y1[0], y2[0]))
    for v, val in enumerate((y1[0], y2[0], y1[1], y2[1])):
        yc[gy, v] = val

    def y_copy(buf, ss, rs, to):
        return pltpu.make_async_remote_copy(
            src_ref=buf.at[gy], dst_ref=buf.at[gy],
            send_sem=ss.at[to], recv_sem=rs.at[gy],
            device_id=(gx, to), device_id_type=MESH)

    def y_all(buf, ss, rs, act):
        for d in range(ny):
            @pl.when(gy != d)
            def _():
                getattr(y_copy(buf, ss, rs, d), act)()

    def y_arrived(buf, ss, rs):
        for d in range(ny):
            @pl.when(gy != d)
            def _():
                pltpu.make_async_remote_copy(
                    src_ref=buf.at[d], dst_ref=buf.at[d],
                    send_sem=ss.at[d], recv_sem=rs.at[d],
                    device_id=(gx, d), device_id_type=MESH).wait_recv()

    y_all(yc, yc_ss, yc_rs, "start")

    def ent_copy(to):
        return pltpu.make_async_remote_copy(
            src_ref=ent_s.at[to], dst_ref=ent_r.at[mine],
            send_sem=ent_ss.at[to], recv_sem=ent_rs.at[mine],
            device_id=(to, gy), device_id_type=MESH)

    def own():
        seg_r[gx] = seg_s[mine]
        for d in range(nx):
            elsewhere(d, pltpu.make_async_remote_copy(
                src_ref=seg_s.at[0], dst_ref=seg_r.at[d],
                send_sem=seg_ss.at[0], recv_sem=seg_rs.at[d],
                device_id=(d, gy), device_id_type=MESH).wait_recv)
        maps = []
        for d in range(nx):
            a, b, c = (seg_r[d, v] for v in range(3))
            maps.append((a, b, c, (1.0 + b * c) / a))
        offs = [(seg_r[d, 3], seg_r[d, 4]) for d in range(nx)]
        long = nx * lx > LONG
        for d, (u, s) in enumerate(join(maps, offs, join_coefs(maps, long), long)):
            ent_s[d, 0] = u
            ent_s[d, 1] = s
        for k in range(half):
            @pl.when(gx != first + k)
            def _():
                ent_copy(first + k).start()
        ent_r[mine] = ent_s[gx]

    if owners < nx:
        pl.when(is_owner)(own)
    else:
        own()

    y_arrived(yc, yc_ss, yc_rs)
    ymaps = [tuple(yc[d, v] for v in range(4)) for d in range(ny)]
    ylong = ny * ly > LONG
    ycoefs = join_coefs(ymaps, ylong)

    for i, val in enumerate(cells):
        for buf, part in zip((fa_v, fb_v, fc_v), val):
            buf[pl.ds(i * ly, ly), :] = part * ivals[i]
    turned = [
        tuple(buf[pl.ds(j, lx, stride=ly), :] for buf in (fa_v, fb_v, fc_v)) for j in range(ly)
    ]
    up, us, qp, qs, weights = one8, zero8, zero8, one8, []
    for j in reversed(range(ly)):
        weights.append((us, qs))
        up, qp = up + sy[j] * us, qp + sy[j] * qs
        us, qs = us + up, qs + qp
    weights = weights[::-1]

    for o in range(groups):
        @pl.when(gx != server + o)
        def _():
            pltpu.make_async_remote_copy(
                src_ref=ent_s.at[0], dst_ref=ent_r.at[o],
                send_sem=ent_ss.at[0], recv_sem=ent_rs.at[o],
                device_id=(server + o, gy), device_id_type=MESH).wait_recv()

    g_y = []
    for j in range(ly):
        o, row = j // rows, pl.ds(j % rows, 1)
        fa, fb, fc = turned[j]
        g_y.append((fa * ent_r[o, 0, row, :] + fb * ent_r[o, 1, row, :]) + fc)
    yo[gy, 0] = -total([w[0] * g for w, g in zip(weights, g_y)])
    yo[gy, 1] = -total([w[1] * g for w, g in zip(weights, g_y)])
    y_all(yo, yo_ss, yo_rs, "start")
    y3, ygs = (zero8, zero8), []
    for j in range(ly):
        y3 = sweep(*y3, sy[j], g_y[j])
        ygs.append(y3[0])

    for o in range(owners):
        elsewhere(base + o, seg_copy(o).wait_send)

    def own_sent():
        for k in range(half):
            @pl.when(gx != first + k)
            def _():
                ent_copy(first + k).wait_send()

    if owners < nx:
        pl.when(is_owner)(own_sent)
    else:
        own_sent()
    y_all(yc, yc_ss, yc_rs, "wait_send")
    y_all(yo, yo_ss, yo_rs, "wait_send")

    y_arrived(yo, yo_ss, yo_rs)
    yoffs = [(yo[d, 0], yo[d, 1]) for d in range(ny)]
    u, s = zero8, zero8
    for d, (du, ds) in enumerate(join(ymaps, yoffs, ycoefs, ylong)):
        here = gy == d
        u, s = jnp.where(here, du, u), jnp.where(here, ds, s)
    for j in range(ly):
        ca, cb = ycells[j]
        out_ref[pl.ds(j, lx, stride=ly), :] = (ca * u + cb * s) + ygs[j]


def solution(mesh):
    nx, ny = mesh.shape["gx"], mesh.shape["gy"]

    def per_device(source, coupling_x, coupling_y, reaction):
        lx, ly, nz = source.shape
        groups = min(nx // 2, ly // 8)
        owners, rows = 2 * groups, ly // groups
        f32 = jnp.float32
        dma = pltpu.SemaphoreType.DMA
        vmem = pl.BlockSpec(memory_space=pltpu.VMEM)
        flat = [
            pltpu.with_memory_space_constraint(a.reshape(lx * ly, nz), pltpu.HBM)
            for a in (source, coupling_x, coupling_y, reaction)
        ]
        out = pl.pallas_call(
            functools.partial(kernel, nx, ny, lx, ly, groups),
            out_shape=jax.ShapeDtypeStruct((lx * ly, nz), f32),
            in_specs=[pl.BlockSpec(memory_space=pltpu.HBM)] * 4,
            out_specs=vmem,
            scratch_shapes=[
                *[pltpu.VMEM((lx * ly, nz), f32)] * 4, dma((4,)),
                pltpu.VMEM((groups, 5, rows, nz), f32),
                pltpu.VMEM((nx, 5, rows, nz), f32),
                pltpu.VMEM((nx, 2, rows, nz), f32),
                pltpu.VMEM((groups, 2, rows, nz), f32),
                pltpu.VMEM((ny, 4, lx, nz), f32),
                pltpu.VMEM((ny, 2, lx, nz), f32),
                *[pltpu.VMEM((lx * ly, nz), f32)] * 4,
                dma((owners,)), dma((nx,)), dma((nx,)), dma((groups,)),
                dma((ny,)), dma((ny,)), dma((ny,)), dma((ny,)),
            ],
            compiler_params=pltpu.CompilerParams(
                collective_id=0, has_side_effects=True, vmem_limit_bytes=16 * 1024 * 1024),
        )(*flat)
        return out.reshape(lx, ly, nz)

    spec = P("gx", "gy", None)
    return jax.shard_map(per_device, mesh=mesh, in_specs=(spec,) * 4, out_specs=spec, check_vma=False)
```

```python
import functools

import jax
import jax.numpy as jnp
from jax import lax
from jax.experimental import pallas as pl
from jax.experimental.pallas import tpu as pltpu
from jax.sharding import PartitionSpec as P

MESH = pl.DeviceIdType.MESH
LONG = 128


def sweep(prev, slope, s, g):
    here = prev + slope
    if g is None:
        return here, slope + s * here
    return here, (slope - g) + s * here


def join_coefs(maps, long):
    one = jnp.ones_like(maps[0][0])
    zero = jnp.zeros_like(one)
    if long:
        ratio, out = zero, []
        for a, b, c, d in maps:
            inv = 1.0 / (c * ratio + d)
            nxt = (a * ratio + b) * inv
            out.append((ratio, inv, nxt))
            ratio = nxt
        return out, 1.0 / (1.0 + ratio)
    hu, hd, out = zero, one, []
    for a, b, c, d in maps:
        out.append((hu, hd))
        hu, hd = a * hu + b * hd, c * hu + d * hd
    return out, 1.0 / (hu + hd)


def join(maps, offs, coefs, long):
    steps, last = coefs
    zero = jnp.zeros_like(last)
    if long:
        sigma, sig = zero, []
        for (a, b, c, d), (p, q), (_, _, nxt) in zip(maps, offs, steps):
            sig.append(sigma)
            sigma = (a * sigma + p) - nxt * (c * sigma + q)
        slope, states = -sigma * last, []
        for k in reversed(range(len(maps))):
            ratio, inv, _ = steps[k]
            slope = (slope - (maps[k][2] * sig[k] + offs[k][1])) * inv
            states.append((ratio * slope + sig[k], slope))
        return states[::-1]
    u, s, part = zero, zero, []
    for (a, b, c, d), (p, q) in zip(maps, offs):
        part.append((u, s))
        u, s = (a * u + b * s) + p, (c * u + d * s) + q
    t = -(u + s) * last
    return [(pu + t * hu, ps + t * hd) for (pu, ps), (hu, hd) in zip(part, steps)]


def total(terms):
    while len(terms) > 1:
        terms = [sum(terms[k + 1:k + 2], terms[k]) for k in range(0, len(terms), 2)]
    return terms[0]


def kernel(nx, ny, lx, ly, groups, f_hbm, kx_hbm, ky_hbm, r_hbm, out_ref,
           f_ref, kx_ref, ky_ref, r_ref, load_sems, seg_s, seg_r, ent_s, ent_r, yc, yo, sy_v, fa_v, fb_v, fc_v,
           seg_ss, seg_rs, ent_ss, ent_rs, yc_ss, yc_rs, yo_ss, yo_rs):
    gx, gy = lax.axis_index("gx"), lax.axis_index("gy")
    rows, half, owners = ly // groups, nx // 2, 2 * groups
    base = half - groups
    upper = (gx >= half).astype(jnp.int32)
    first = upper * half
    server = base + upper * groups
    mine = lax.rem(gx + (nx * groups - base), groups)
    is_owner = (gx >= base) & (gx < base + owners)

    def elsewhere(d, act):
        if base <= d < base + owners:
            pl.when(gx != d)(lambda: act() and None)
        else:
            act()

    barrier = pltpu.get_barrier_semaphore()

    loads = [
        pltpu.make_async_copy(src, dst, load_sems.at[n])
        for n, (src, dst) in enumerate(
            ((kx_hbm, kx_ref), (r_hbm, r_ref), (f_hbm, f_ref), (ky_hbm, ky_ref)))
    ]
    for load in loads:
        load.start()

    @pl.when(is_owner)
    def _():
        for k in range(1, nx):
            pl.semaphore_signal(barrier, inc=1, device_id=(lax.rem(gx + k, nx), gy), device_id_type=MESH)

    for k in range(1, ny):
        pl.semaphore_signal(barrier, inc=1, device_id=(gx, lax.rem(gy + k, ny)), device_id_type=MESH)
    for load in loads[:3]:
        load.wait()

    one = jnp.ones((ly, f_ref.shape[1]), jnp.float32)
    zero = jnp.zeros_like(one)
    h1, h2, h3 = (one, zero), (zero, one), (zero, zero)
    cells = []
    for i in range(lx):
        at = pl.ds(i * ly, ly)
        inv = 1.0 / kx_ref[at, :]
        s, g = r_ref[at, :] * inv, f_ref[at, :] * inv
        h1, h2, h3 = sweep(*h1, s, None), sweep(*h2, s, None), sweep(*h3, s, g)
        cells.append((h1[0], h2[0], h3[0]))
    for v, val in enumerate((h1[0], h2[0], h1[1], h3[0], h3[1])):
        for o in range(groups):
            seg_s[o, v] = val[o * rows:(o + 1) * rows, :]

    pl.semaphore_wait(barrier, owners + ny - 1 - is_owner.astype(jnp.int32))

    def seg_copy(o):
        return pltpu.make_async_remote_copy(
            src_ref=seg_s.at[o % groups], dst_ref=seg_r.at[gx],
            send_sem=seg_ss.at[o], recv_sem=seg_rs.at[gx],
            device_id=(base + o, gy), device_id_type=MESH)

    for o in range(owners):
        elsewhere(base + o, seg_copy(o).start)

    loads[3].wait()

    ivals = []
    for i in range(lx):
        at = pl.ds(i * ly, ly)
        inv = 1.0 / ky_ref[at, :]
        ivals.append(inv)
        sy_v[at, :] = r_ref[at, :] * inv
    one8 = jnp.ones((lx, f_ref.shape[1]), jnp.float32)
    zero8 = jnp.zeros_like(one8)
    y1, y2, ycells, sy = (one8, zero8), (zero8, one8), [], []
    for j in range(ly):
        s = sy_v[pl.ds(j, lx, stride=ly), :]
        sy.append(s)
        y1, y2 = sweep(*y1, s, None), sweep(*y2, s, None)
        ycells.append((y1[0], y2[0]))
    for v, val in enumerate((y1[0], y2[0], y1[1], y2[1])):
        yc[gy, v] = val

    def y_copy(buf, ss, rs, to):
        return pltpu.make_async_remote_copy(
            src_ref=buf.at[gy], dst_ref=buf.at[gy],
            send_sem=ss.at[to], recv_sem=rs.at[gy],
            device_id=(gx, to), device_id_type=MESH)

    def y_all(buf, ss, rs, act):
        for d in range(ny):
            @pl.when(gy != d)
            def _():
                getattr(y_copy(buf, ss, rs, d), act)()

    def y_arrived(buf, ss, rs):
        for d in range(ny):
            @pl.when(gy != d)
            def _():
                pltpu.make_async_remote_copy(
                    src_ref=buf.at[d], dst_ref=buf.at[d],
                    send_sem=ss.at[d], recv_sem=rs.at[d],
                    device_id=(gx, d), device_id_type=MESH).wait_recv()

    y_all(yc, yc_ss, yc_rs, "start")

    def ent_copy(to):
        return pltpu.make_async_remote_copy(
            src_ref=ent_s.at[to], dst_ref=ent_r.at[mine],
            send_sem=ent_ss.at[to], recv_sem=ent_rs.at[mine],
            device_id=(to, gy), device_id_type=MESH)

    def own():
        seg_r[gx] = seg_s[mine]
        for d in range(nx):
            elsewhere(d, pltpu.make_async_remote_copy(
                src_ref=seg_s.at[0], dst_ref=seg_r.at[d],
                send_sem=seg_ss.at[0], recv_sem=seg_rs.at[d],
                device_id=(d, gy), device_id_type=MESH).wait_recv)
        maps = []
        for d in range(nx):
            a, b, c = (seg_r[d, v] for v in range(3))
            maps.append((a, b, c, (1.0 + b * c) / a))
        offs = [(seg_r[d, 3], seg_r[d, 4]) for d in range(nx)]
        long = nx * lx > LONG
        for d, (u, s) in enumerate(join(maps, offs, join_coefs(maps, long), long)):
            ent_s[d, 0] = u
            ent_s[d, 1] = s
        for k in range(half):
            @pl.when(gx != first + k)
            def _():
                ent_copy(first + k).start()
        ent_r[mine] = ent_s[gx]

    if owners < nx:
        pl.when(is_owner)(own)
    else:
        own()

    y_arrived(yc, yc_ss, yc_rs)
    ymaps = [tuple(yc[d, v] for v in range(4)) for d in range(ny)]
    ylong = ny * ly > LONG
    ycoefs = join_coefs(ymaps, ylong)

    for i, val in enumerate(cells):
        for buf, part in zip((fa_v, fb_v, fc_v), val):
            buf[pl.ds(i * ly, ly), :] = part * ivals[i]
    turned = [
        tuple(buf[pl.ds(j, lx, stride=ly), :] for buf in (fa_v, fb_v, fc_v)) for j in range(ly)
    ]
    up, us, qp, qs, weights = one8, zero8, zero8, one8, []
    for j in reversed(range(ly)):
        weights.append((us, qs))
        up, qp = up + sy[j] * us, qp + sy[j] * qs
        us, qs = us + up, qs + qp
    weights = weights[::-1]

    for o in range(groups):
        @pl.when(gx != server + o)
        def _():
            pltpu.make_async_remote_copy(
                src_ref=ent_s.at[0], dst_ref=ent_r.at[o],
                send_sem=ent_ss.at[0], recv_sem=ent_rs.at[o],
                device_id=(server + o, gy), device_id_type=MESH).wait_recv()

    g_y = []
    for j in range(ly):
        o, row = j // rows, pl.ds(j % rows, 1)
        fa, fb, fc = turned[j]
        g_y.append((fa * ent_r[o, 0, row, :] + fb * ent_r[o, 1, row, :]) + fc)
    yo[gy, 0] = -total([w[0] * g for w, g in zip(weights, g_y)])
    yo[gy, 1] = -total([w[1] * g for w, g in zip(weights, g_y)])
    y_all(yo, yo_ss, yo_rs, "start")
    y3, ygs = (zero8, zero8), []
    for j in range(ly):
        y3 = sweep(*y3, sy[j], g_y[j])
        ygs.append(y3[0])

    for o in range(owners):
        elsewhere(base + o, seg_copy(o).wait_send)

    def own_sent():
        for k in range(half):
            @pl.when(gx != first + k)
            def _():
                ent_copy(first + k).wait_send()

    if owners < nx:
        pl.when(is_owner)(own_sent)
    else:
        own_sent()
    y_all(yc, yc_ss, yc_rs, "wait_send")
    y_all(yo, yo_ss, yo_rs, "wait_send")

    y_arrived(yo, yo_ss, yo_rs)
    yoffs = [(yo[d, 0], yo[d, 1]) for d in range(ny)]
    u, s = zero8, zero8
    for d, (du, ds) in enumerate(join(ymaps, yoffs, ycoefs, ylong)):
        here = gy == d
        u, s = jnp.where(here, du, u), jnp.where(here, ds, s)
    for j in range(ly):
        ca, cb = ycells[j]
        out_ref[pl.ds(j, lx, stride=ly), :] = (ca * u + cb * s) + ygs[j]


def solution(mesh):
    nx, ny = mesh.shape["gx"], mesh.shape["gy"]

    def per_device(source, coupling_x, coupling_y, reaction):
        lx, ly, nz = source.shape
        groups = max(1, min(nx // 2, ly // 16))
        owners, rows = 2 * groups, ly // groups
        f32 = jnp.float32
        dma = pltpu.SemaphoreType.DMA
        vmem = pl.BlockSpec(memory_space=pltpu.VMEM)
        flat = [
            pltpu.with_memory_space_constraint(a.reshape(lx * ly, nz), pltpu.HBM)
            for a in (source, coupling_x, coupling_y, reaction)
        ]
        out = pl.pallas_call(
            functools.partial(kernel, nx, ny, lx, ly, groups),
            out_shape=jax.ShapeDtypeStruct((lx * ly, nz), f32),
            in_specs=[pl.BlockSpec(memory_space=pltpu.HBM)] * 4,
            out_specs=vmem,
            scratch_shapes=[
                *[pltpu.VMEM((lx * ly, nz), f32)] * 4, dma((4,)),
                pltpu.VMEM((groups, 5, rows, nz), f32),
                pltpu.VMEM((nx, 5, rows, nz), f32),
                pltpu.VMEM((nx, 2, rows, nz), f32),
                pltpu.VMEM((groups, 2, rows, nz), f32),
                pltpu.VMEM((ny, 4, lx, nz), f32),
                pltpu.VMEM((ny, 2, lx, nz), f32),
                *[pltpu.VMEM((lx * ly, nz), f32)] * 4,
                dma((owners,)), dma((nx,)), dma((nx,)), dma((groups,)),
                dma((ny,)), dma((ny,)), dma((ny,)), dma((ny,)),
            ],
            compiler_params=pltpu.CompilerParams(
                collective_id=0, has_side_effects=True, vmem_limit_bytes=16 * 1024 * 1024),
        )(*flat)
        return out.reshape(lx, ly, nz)

    spec = P("gx", "gy", None)
    return jax.shard_map(per_device, mesh=mesh, in_specs=(spec,) * 4, out_specs=spec, check_vma=False)
```

```python
import functools

import jax
import jax.numpy as jnp
from jax import lax
from jax.experimental import pallas as pl
from jax.experimental.pallas import tpu as pltpu
from jax.sharding import PartitionSpec as P

MESH = pl.DeviceIdType.MESH
LONG = 128


def sweep(prev, slope, s, g):
    here = prev + slope
    if g is None:
        return here, slope + s * here
    return here, (slope - g) + s * here


def join_coefs(maps, long):
    one = jnp.ones_like(maps[0][0])
    zero = jnp.zeros_like(one)
    if long:
        ratio, out = zero, []
        for a, b, c, d in maps:
            inv = 1.0 / (c * ratio + d)
            nxt = (a * ratio + b) * inv
            out.append((ratio, inv, nxt))
            ratio = nxt
        return out, 1.0 / (1.0 + ratio)
    hu, hd, out = zero, one, []
    for a, b, c, d in maps:
        out.append((hu, hd))
        hu, hd = a * hu + b * hd, c * hu + d * hd
    return out, 1.0 / (hu + hd)


def join(maps, offs, coefs, long):
    steps, last = coefs
    zero = jnp.zeros_like(last)
    if long:
        sigma, sig = zero, []
        for (a, b, c, d), (p, q), (_, _, nxt) in zip(maps, offs, steps):
            sig.append(sigma)
            sigma = (a * sigma + p) - nxt * (c * sigma + q)
        slope, states = -sigma * last, []
        for k in reversed(range(len(maps))):
            ratio, inv, _ = steps[k]
            slope = (slope - (maps[k][2] * sig[k] + offs[k][1])) * inv
            states.append((ratio * slope + sig[k], slope))
        return states[::-1]
    u, s, part = zero, zero, []
    for (a, b, c, d), (p, q) in zip(maps, offs):
        part.append((u, s))
        u, s = (a * u + b * s) + p, (c * u + d * s) + q
    t = -(u + s) * last
    return [(pu + t * hu, ps + t * hd) for (pu, ps), (hu, hd) in zip(part, steps)]


def total(terms):
    while len(terms) > 1:
        terms = [sum(terms[k + 1:k + 2], terms[k]) for k in range(0, len(terms), 2)]
    return terms[0]


def kernel(nx, ny, lx, ly, groups, f_hbm, kx_hbm, ky_hbm, r_hbm, out_ref,
           f_ref, kx_ref, ky_ref, r_ref, load_sems, seg_s, seg_r, ent_s, ent_r, yc, yo, sy_v, fa_v, fb_v, fc_v,
           seg_ss, seg_rs, ent_ss, ent_rs, yc_ss, yc_rs, yo_ss, yo_rs):
    gx, gy = lax.axis_index("gx"), lax.axis_index("gy")
    rows, half, owners = ly // groups, nx // 2, 2 * groups
    base = half - groups
    upper = (gx >= half).astype(jnp.int32)
    first = upper * half
    server = base + upper * groups
    mine = lax.rem(gx + (nx * groups - base), groups)
    is_owner = (gx >= base) & (gx < base + owners)

    def elsewhere(d, act):
        if base <= d < base + owners:
            pl.when(gx != d)(lambda: act() and None)
        else:
            act()

    barrier = pltpu.get_barrier_semaphore()

    loads = [
        pltpu.make_async_copy(src, dst, load_sems.at[n])
        for n, (src, dst) in enumerate(
            ((kx_hbm, kx_ref), (r_hbm, r_ref), (f_hbm, f_ref), (ky_hbm, ky_ref)))
    ]
    for load in loads:
        load.start()

    @pl.when(is_owner)
    def _():
        for k in range(1, nx):
            pl.semaphore_signal(barrier, inc=1, device_id=(lax.rem(gx + k, nx), gy), device_id_type=MESH)

    for k in range(1, ny):
        pl.semaphore_signal(barrier, inc=1, device_id=(gx, lax.rem(gy + k, ny)), device_id_type=MESH)
    for load in loads[:3]:
        load.wait()

    one = jnp.ones((ly, f_ref.shape[1]), jnp.float32)
    zero = jnp.zeros_like(one)
    h1, h2, h3 = (one, zero), (zero, one), (zero, zero)
    cells = []
    for i in range(lx):
        at = pl.ds(i * ly, ly)
        inv = 1.0 / kx_ref[at, :]
        s, g = r_ref[at, :] * inv, f_ref[at, :] * inv
        h1, h2, h3 = sweep(*h1, s, None), sweep(*h2, s, None), sweep(*h3, s, g)
        cells.append((h1[0], h2[0], h3[0]))
    for v, val in enumerate((h1[0], h2[0], h1[1], h3[0], h3[1])):
        for o in range(groups):
            seg_s[o, v] = val[o * rows:(o + 1) * rows, :]

    pl.semaphore_wait(barrier, owners + ny - 1 - is_owner.astype(jnp.int32))

    def seg_copy(o):
        return pltpu.make_async_remote_copy(
            src_ref=seg_s.at[o % groups], dst_ref=seg_r.at[gx],
            send_sem=seg_ss.at[o], recv_sem=seg_rs.at[gx],
            device_id=(base + o, gy), device_id_type=MESH)

    for o in range(owners):
        elsewhere(base + o, seg_copy(o).start)

    loads[3].wait()

    ivals = []
    for i in range(lx):
        at = pl.ds(i * ly, ly)
        inv = 1.0 / ky_ref[at, :]
        ivals.append(inv)
        sy_v[at, :] = r_ref[at, :] * inv
    one8 = jnp.ones((lx, f_ref.shape[1]), jnp.float32)
    zero8 = jnp.zeros_like(one8)
    y1, y2, ycells, sy = (one8, zero8), (zero8, one8), [], []
    for j in range(ly):
        s = sy_v[pl.ds(j, lx, stride=ly), :]
        sy.append(s)
        y1, y2 = sweep(*y1, s, None), sweep(*y2, s, None)
        ycells.append((y1[0], y2[0]))
    for v, val in enumerate((y1[0], y2[0], y1[1])):
        yc[gy, v] = val

    def y_copy(buf, ss, rs, to):
        return pltpu.make_async_remote_copy(
            src_ref=buf.at[gy], dst_ref=buf.at[gy],
            send_sem=ss.at[to], recv_sem=rs.at[gy],
            device_id=(gx, to), device_id_type=MESH)

    def y_all(buf, ss, rs, act):
        for d in range(ny):
            @pl.when(gy != d)
            def _():
                getattr(y_copy(buf, ss, rs, d), act)()

    def y_arrived(buf, ss, rs):
        for d in range(ny):
            @pl.when(gy != d)
            def _():
                pltpu.make_async_remote_copy(
                    src_ref=buf.at[d], dst_ref=buf.at[d],
                    send_sem=ss.at[d], recv_sem=rs.at[d],
                    device_id=(gx, d), device_id_type=MESH).wait_recv()

    y_all(yc, yc_ss, yc_rs, "start")

    def ent_copy(to):
        return pltpu.make_async_remote_copy(
            src_ref=ent_s.at[to], dst_ref=ent_r.at[mine],
            send_sem=ent_ss.at[to], recv_sem=ent_rs.at[mine],
            device_id=(to, gy), device_id_type=MESH)

    def own():
        seg_r[gx] = seg_s[mine]
        for d in range(nx):
            elsewhere(d, pltpu.make_async_remote_copy(
                src_ref=seg_s.at[0], dst_ref=seg_r.at[d],
                send_sem=seg_ss.at[0], recv_sem=seg_rs.at[d],
                device_id=(d, gy), device_id_type=MESH).wait_recv)
        maps = []
        for d in range(nx):
            a, b, c = (seg_r[d, v] for v in range(3))
            maps.append((a, b, c, (1.0 + b * c) / a))
        offs = [(seg_r[d, 3], seg_r[d, 4]) for d in range(nx)]
        long = nx * lx > LONG
        for d, (u, s) in enumerate(join(maps, offs, join_coefs(maps, long), long)):
            ent_s[d, 0] = u
            ent_s[d, 1] = s
        for k in range(half):
            @pl.when(gx != first + k)
            def _():
                ent_copy(first + k).start()
        ent_r[mine] = ent_s[gx]

    if owners < nx:
        pl.when(is_owner)(own)
    else:
        own()

    y_arrived(yc, yc_ss, yc_rs)
    ymaps = []
    for d in range(ny):
        a, b, c = (yc[d, v] for v in range(3))
        ymaps.append((a, b, c, (1.0 + b * c) / a))
    ylong = ny * ly > LONG
    ycoefs = join_coefs(ymaps, ylong)

    for i, val in enumerate(cells):
        for buf, part in zip((fa_v, fb_v, fc_v), val):
            buf[pl.ds(i * ly, ly), :] = part * ivals[i]
    turned = [
        tuple(buf[pl.ds(j, lx, stride=ly), :] for buf in (fa_v, fb_v, fc_v)) for j in range(ly)
    ]
    up, us, qp, qs, weights = one8, zero8, zero8, one8, []
    for j in reversed(range(ly)):
        weights.append((us, qs))
        up, qp = up + sy[j] * us, qp + sy[j] * qs
        us, qs = us + up, qs + qp
    weights = weights[::-1]

    for o in range(groups):
        @pl.when(gx != server + o)
        def _():
            pltpu.make_async_remote_copy(
                src_ref=ent_s.at[0], dst_ref=ent_r.at[o],
                send_sem=ent_ss.at[0], recv_sem=ent_rs.at[o],
                device_id=(server + o, gy), device_id_type=MESH).wait_recv()

    g_y = []
    for j in range(ly):
        o, row = j // rows, pl.ds(j % rows, 1)
        fa, fb, fc = turned[j]
        g_y.append((fa * ent_r[o, 0, row, :] + fb * ent_r[o, 1, row, :]) + fc)
    yo[gy, 0] = -total([w[0] * g for w, g in zip(weights, g_y)])
    yo[gy, 1] = -total([w[1] * g for w, g in zip(weights, g_y)])
    y_all(yo, yo_ss, yo_rs, "start")
    y3, ygs = (zero8, zero8), []
    for j in range(ly):
        y3 = sweep(*y3, sy[j], g_y[j])
        ygs.append(y3[0])

    for o in range(owners):
        elsewhere(base + o, seg_copy(o).wait_send)

    def own_sent():
        for k in range(half):
            @pl.when(gx != first + k)
            def _():
                ent_copy(first + k).wait_send()

    if owners < nx:
        pl.when(is_owner)(own_sent)
    else:
        own_sent()
    y_all(yc, yc_ss, yc_rs, "wait_send")
    y_all(yo, yo_ss, yo_rs, "wait_send")

    y_arrived(yo, yo_ss, yo_rs)
    yoffs = [(yo[d, 0], yo[d, 1]) for d in range(ny)]
    u, s = zero8, zero8
    for d, (du, ds) in enumerate(join(ymaps, yoffs, ycoefs, ylong)):
        here = gy == d
        u, s = jnp.where(here, du, u), jnp.where(here, ds, s)
    for j in range(ly):
        ca, cb = ycells[j]
        out_ref[pl.ds(j, lx, stride=ly), :] = (ca * u + cb * s) + ygs[j]


def solution(mesh):
    nx, ny = mesh.shape["gx"], mesh.shape["gy"]

    def per_device(source, coupling_x, coupling_y, reaction):
        lx, ly, nz = source.shape
        groups = max(1, min(nx // 2, ly // 16))
        owners, rows = 2 * groups, ly // groups
        f32 = jnp.float32
        dma = pltpu.SemaphoreType.DMA
        vmem = pl.BlockSpec(memory_space=pltpu.VMEM)
        flat = [
            pltpu.with_memory_space_constraint(a.reshape(lx * ly, nz), pltpu.HBM)
            for a in (source, coupling_x, coupling_y, reaction)
        ]
        out = pl.pallas_call(
            functools.partial(kernel, nx, ny, lx, ly, groups),
            out_shape=jax.ShapeDtypeStruct((lx * ly, nz), f32),
            in_specs=[pl.BlockSpec(memory_space=pltpu.HBM)] * 4,
            out_specs=vmem,
            scratch_shapes=[
                *[pltpu.VMEM((lx * ly, nz), f32)] * 4, dma((4,)),
                pltpu.VMEM((groups, 5, rows, nz), f32),
                pltpu.VMEM((nx, 5, rows, nz), f32),
                pltpu.VMEM((nx, 2, rows, nz), f32),
                pltpu.VMEM((groups, 2, rows, nz), f32),
                pltpu.VMEM((ny, 3, lx, nz), f32),
                pltpu.VMEM((ny, 2, lx, nz), f32),
                *[pltpu.VMEM((lx * ly, nz), f32)] * 4,
                dma((owners,)), dma((nx,)), dma((nx,)), dma((groups,)),
                dma((ny,)), dma((ny,)), dma((ny,)), dma((ny,)),
            ],
            compiler_params=pltpu.CompilerParams(
                collective_id=0, has_side_effects=True, vmem_limit_bytes=16 * 1024 * 1024),
        )(*flat)
        return out.reshape(lx, ly, nz)

    spec = P("gx", "gy", None)
    return jax.shard_map(per_device, mesh=mesh, in_specs=(spec,) * 4, out_specs=spec, check_vma=False)
```
